32 devices in a mesh: dp: 8 (over y, x, core), tensor: 4 (over z).
Axes of the slice: x: 2, y: 2, z: 4, core: 2. Of those that a mesh axis runs over, the one named last changes fastest.
Arguments:
- layer_input: bfloat16 [16384, 768], P(('dp', 'tensor')), may hold values from -6 to 6
- cotangent: bfloat16 [16384, 768], P(('dp', 'tensor')), may hold values from -6 to 6
- lengths: int32 [8, 6], P('dp'), may hold values from 0 to 2048, as said below
- w_qkv: bfloat16 [768, 3, 768], P('dp', None, 'tensor'), may hold values from -0.21875 to 0.21875
- w_out: bfloat16 [768, 768], P('tensor', 'dp'), may hold values from -3.5 to 3.5
- w_in: bfloat16 [768, 2, 1152], P('dp', None, 'tensor'), may hold values from -0.21875 to 0.21875
- w_down: bfloat16 [1152, 768], P('tensor', 'dp'), may hold values from -0.1875 to 0.1875
- attn_gain: bfloat16 [768], P('dp'), may hold values from 0.5 to 1.5
- mlp_gain: bfloat16 [768], P('dp'), may hold values from 0.5 to 1.5
Outputs:
- output: bfloat16 [16384, 768], P(('dp', 'tensor'))
- grad_input: float32 [16384, 768], P(('dp', 'tensor'))
- grad_w_qkv: float32 [768, 3, 768], P('dp', None, 'tensor')
- grad_w_out: float32 [768, 768], P('tensor', 'dp')
- grad_w_in: float32 [768, 2, 1152], P('dp', None, 'tensor')
- grad_w_down: float32 [1152, 768], P('tensor', 'dp')
- grad_attn_gain: float32 [768], P(('dp', 'tensor'))
- grad_mlp_gain: float32 [768], P(('dp', 'tensor'))
The draws below stay inside these ranges and needn't reach their ends.
Inputs may be any that keep to these rules, and one draw needn't show every extreme that they name: `lengths`: each row sums to 2048. The third entry of each row is a document that starts within the first quarter of the group's tokens and ends within its last quarter; other entries may be zero.
All inputs are finite; a program needn't handle non-finite values.
Results may differ from the reference program's by a relative error of at most 0.02.
Values may be sent and summed in bfloat16 or wider, within the bound.
A program may use at most 128 MiB of HBM per device.

```python
import math
import jax
import jax.numpy as jnp
from jax import lax

D = 768
HEADS = 12
HEAD_DIM = 64
FF = 1152
GROUP_ROWS = 2048
TOKENS = 16384


def draw_lengths(key, part):
    key = jax.random.fold_in(key, 11)
    group_count = TOKENS // GROUP_ROWS
    quarter = GROUP_ROWS // 4
    keys_all = jax.random.split(key, 6)
    before = jax.random.randint(keys_all[0], (group_count,), 0, quarter)
    longest = jax.random.randint(keys_all[1], (group_count,), 3 * quarter - before + 1, GROUP_ROWS - before + 1)
    chosen = jax.random.randint(keys_all[2], (), 0, group_count)
    whole_group = jnp.arange(group_count) == chosen
    before = jnp.where(whole_group, 0, before)
    longest = jnp.where(whole_group, GROUP_ROWS, longest)
    after = GROUP_ROWS - before - longest
    first_len = jax.random.randint(keys_all[3], (group_count,), 0, before + 1)
    second_len = before - first_len
    third_len = jax.random.randint(keys_all[4], (group_count,), 0, after + 1)
    remain = after - third_len
    fourth_len = jax.random.randint(keys_all[5], (group_count,), 0, remain + 1)
    fifth_len = remain - fourth_len
    return jnp.stack([first_len, second_len, longest, third_len, fourth_len, fifth_len], axis=-1).astype(jnp.int32)


def with_spikes(drawn, own_key, source, target, shards_of, factor):
    def block_of(dim):
        return (jnp.arange(drawn.shape[dim]) // (drawn.shape[dim] // shards_of)).reshape((-1,) + (1,) * (drawn.ndim - 1 - dim))

    first = jax.random.permutation(own_key, shards_of)[block_of(target)]
    other_side = (block_of(target) + shards_of // 2) % shards_of
    return jnp.where((block_of(source) == first) | (block_of(source) == other_side), factor * drawn, drawn)


def block_scale(stream_key, shape, cuts, low, top_value):
    loudness = 1.0
    for axis_at, parts in cuts:
        steps = jax.random.uniform(jax.random.fold_in(jax.random.fold_in(stream_key, 6), axis_at), (parts,), jnp.float32, low / len(cuts), top_value / len(cuts))
        loudness = loudness * jnp.repeat(jnp.exp(steps), shape[axis_at] // parts).reshape((-1,) + (1,) * (len(shape) - 1 - axis_at))
    return loudness


def normal_values(rng, shape, scale, reach, cuts=(), held_as=jnp.bfloat16):
    drawn = scale * jax.random.normal(rng, shape, jnp.float32)
    if cuts:
        drawn = drawn * block_scale(rng, shape, cuts, -0.22, 0.18)
    return jnp.clip(drawn, -reach, reach).astype(held_as)


def heavy_noise(rng, shape, deviation, bound, cuts, heavy, held_as=jnp.bfloat16):
    values = deviation * jax.random.normal(rng, shape, jnp.float32)
    if cuts:
        values = values * block_scale(rng, shape, cuts, -0.22, 0.18)
    return jnp.clip(with_spikes(values, jax.random.fold_in(rng, 3), *heavy), -bound, bound).astype(held_as)


def setup_inputs(seed: int = 0) -> dict:
    streams_of = jax.random.split(jax.random.key(seed), 10)
    layer_input = heavy_noise(streams_of[0], (TOKENS, D), 1.0, 6.0, ((0, 32),), (0, 1, 32, 2.75))
    cotangent = heavy_noise(streams_of[1], (TOKENS, D), 1.0, 6.0, ((0, 32),), (0, 1, 32, 2.75))
    lengths = draw_lengths(jax.random.fold_in(streams_of[9], 71), 0)
    w_qkv = normal_values(streams_of[3], (D, 3, D), D ** -0.5, 0.21875, ((0, 8), (2, 4)))
    w_out = normal_values(streams_of[4], (D, D), (max(D * 8 // GROUP_ROWS, 1)) ** -0.5, 3.5, ((0, 4), (1, 8)))
    w_in = normal_values(streams_of[5], (D, 2, FF), D ** -0.5, 0.21875, ((0, 8), (2, 4)))
    w_down = normal_values(streams_of[6], (FF, D), FF ** -0.5, 0.1875, ((0, 4), (1, 8)))
    attn_gain = jnp.clip(1.0 + 0.1 * jax.random.normal(streams_of[7], (D,), jnp.float32), 0.5, 1.5).astype(jnp.bfloat16)
    mlp_gain = jnp.clip(1.0 + 0.1 * jax.random.normal(streams_of[8], (D,), jnp.float32), 0.5, 1.5).astype(jnp.bfloat16)
    return dict(layer_input=layer_input, cotangent=cotangent, lengths=lengths, w_qkv=w_qkv, w_out=w_out, w_in=w_in, w_down=w_down, attn_gain=attn_gain, mlp_gain=mlp_gain)


NORM_EPS = 1e-05
ROPE_BASE = 160000.0
MASKED_SCORE = -1e+30
HIGHEST = lax.Precision.HIGHEST

@jax.custom_vjp
def low(v):
    return lax.optimization_barrier(v.astype(jnp.bfloat16)).astype(jnp.float32)

@jax.custom_vjp
def low_back(v):
    return v

def low_keep(v):
    return (low(v), None)

def low_pass(kept, grad):
    return (grad,)

def back_keep(v):
    return (v, None)

def back_low(kept, grad):
    return (low(grad),)
low.defvjp(low_keep, low_pass)
low_back.defvjp(back_keep, back_low)

def layer_norm(values_in, gain):
    center = lax.optimization_barrier(jnp.mean(values_in, axis=-1, keepdims=True))
    shifted = values_in - center
    spread = lax.optimization_barrier(jnp.mean(shifted * shifted, axis=-1, keepdims=True))
    return shifted * lax.rsqrt(spread + NORM_EPS) * gain

def layout(lengths_row, row_count):
    doc_ends = jnp.cumsum(lengths_row).astype(jnp.int32)
    doc_starts = doc_ends - lengths_row
    row_index = jnp.arange(row_count, dtype=jnp.int32)
    segment = lax.optimization_barrier(jnp.sum((row_index[:, None] >= doc_ends[None, :]).astype(jnp.int32), axis=1))
    slot_ids = jnp.arange(lengths_row.shape[0], dtype=jnp.int32)
    start_of = lax.optimization_barrier(jnp.sum(jnp.where(segment[:, None] == slot_ids[None, :], doc_starts[None, :], 0), axis=1))
    return (segment, (row_index - start_of).astype(jnp.int32))

def rotate(vectors, position):
    half_dim = vectors.shape[-1] // 2
    pair_ids = jnp.arange(half_dim, dtype=jnp.float32)
    inverse = jnp.exp(pair_ids * (-2.0 * math.log(ROPE_BASE) / vectors.shape[-1]))
    angles = position.astype(jnp.float32)[:, None] * inverse[None, :]
    cosine = jnp.cos(angles)[:, None, :]
    sine = jnp.sin(angles)[:, None, :]
    first = vectors[..., :half_dim]
    second = vectors[..., half_dim:]
    return jnp.concatenate([first * cosine - second * sine, second * cosine + first * sine], axis=-1)

def attend_block(query_blk, segment_blk, key_all, value_all, segment):
    scores = jnp.einsum('qhd,khd->hqk', query_blk, key_all, precision=HIGHEST) * HEAD_DIM ** (-0.5)
    scores = low_back(scores)
    allowed = (segment_blk[:, None] == segment[None, :])[None, :, :]
    scores = jnp.where(allowed, scores, MASKED_SCORE)
    peak = lax.optimization_barrier(jnp.max(scores, axis=-1, keepdims=True))
    log_total = peak + jnp.log(lax.optimization_barrier(jnp.sum(jnp.exp(scores - peak), axis=-1, keepdims=True)))
    weights = jnp.exp(scores - log_total)
    return jnp.einsum('hqk,khd->qhd', low(weights), value_all, precision=HIGHEST)

def layer(input_rows, w_qkv, w_out, w_in, w_down, attn_gain, mlp_gain, segment, position):
    row_count = input_rows.shape[0]
    normed_one = low(layer_norm(input_rows, attn_gain))
    projected = jnp.dot(normed_one, w_qkv.reshape(D, 3 * D), precision=HIGHEST)
    projected = projected.reshape(row_count, 3, HEADS, HEAD_DIM)
    queries = low(rotate(low_back(projected[:, 0]), position))
    key_rows = low(rotate(low_back(projected[:, 1]), position))
    value_rows = low(low_back(projected[:, 2]))
    block_len = min(512, row_count)
    block_count = row_count // block_len

    def block_step(pieces):
        return attend_block(pieces[0], pieces[1], key_rows, value_rows, segment)
    heads_out = lax.map(jax.checkpoint(block_step), (queries.reshape(block_count, block_len, HEADS, HEAD_DIM), segment.reshape(block_count, block_len)))
    mixed = low(low_back(heads_out.reshape(row_count, D)))
    attention = low_back(jnp.dot(mixed, w_out, precision=HIGHEST))
    hidden = input_rows + attention
    normed_two = low(layer_norm(hidden, mlp_gain))
    gate_up = jnp.dot(normed_two, w_in.reshape(D, 2 * FF), precision=HIGHEST).reshape(row_count, 2, FF)
    activated = low(jax.nn.gelu(low_back(gate_up[:, 0]), approximate=False) * low_back(gate_up[:, 1]))
    branch = low_back(jnp.dot(activated, w_down, precision=HIGHEST))
    return hidden + branch

def reference(layer_input, cotangent, lengths, w_qkv, w_out, w_in, w_down, attn_gain, mlp_gain):
    group_count = layer_input.shape[0] // GROUP_ROWS
    params_f32 = (w_qkv.astype(jnp.float32), w_out.astype(jnp.float32), w_in.astype(jnp.float32), w_down.astype(jnp.float32), attn_gain.astype(jnp.float32), mlp_gain.astype(jnp.float32))

    def one_group(running, pieces):
        input_rows, cot_rows, length_row = pieces
        segment, position = layout(length_row, GROUP_ROWS)

        def forward(rows_in, *params):
            return layer(rows_in, *params, segment, position)
        result, pullback = jax.vjp(forward, input_rows.astype(jnp.float32), *params_f32)
        grads = pullback(cot_rows.astype(jnp.float32))
        updated = tuple((before + fresh for before, fresh in zip(running, grads[1:])))
        return (updated, (result.astype(jnp.bfloat16), grads[0]))
    start_sums = tuple((jnp.zeros(weight_f32.shape, jnp.float32) for weight_f32 in params_f32))
    sums, (outputs, grad_rows) = lax.scan(one_group, start_sums, (layer_input.reshape(group_count, GROUP_ROWS, D), cotangent.reshape(group_count, GROUP_ROWS, D), lengths))
    return (outputs.reshape(-1, D), grad_rows.reshape(-1, D), sums[0], sums[1], sums[2], sums[3], sums[4], sums[5])
```

```python
import math

import jax
import jax.numpy as jnp
from jax import lax
from jax.experimental import pallas as pl
from jax.experimental.pallas import tpu as pltpu
from jax.sharding import PartitionSpec as P

HEAD_DIM = 64


NORM_EPS = 1e-05
ROPE_BASE = 160000.0
MASKED_SCORE = -1e30
VMEM_BYTES = 48 * 1024 * 1024
FORWARD_BLOCK = 512
BACKWARD_BLOCK = 512


def in_blocks(shard, dim, size):
    shape = shard.shape
    parts = shard.reshape(*shape[:dim], size, shape[dim] // size, *shape[dim + 1 :])
    return jnp.moveaxis(parts, dim, 0)


def sent_and_summed(shard, axis, dim):
    parts = in_blocks(shard, dim, lax.axis_size(axis))
    arrived = lax.all_to_all(parts, axis, split_axis=0, concat_axis=0, tiled=True)
    return arrived.astype(jnp.float32).sum(axis=0)


def layer_norm(values_in, gain):
    center = jnp.mean(values_in, axis=-1, keepdims=True)
    shifted = values_in - center
    spread = jnp.mean(shifted * shifted, axis=-1, keepdims=True)
    return shifted * lax.rsqrt(spread + NORM_EPS) * gain


def layout(lengths_row, row_count):
    doc_ends = jnp.cumsum(lengths_row)
    doc_starts = doc_ends - lengths_row
    row_index = jnp.arange(row_count, dtype=jnp.int32)
    segment = jnp.sum((row_index[:, None] >= doc_ends[None, :]).astype(jnp.int32), axis=1)
    slot_ids = jnp.arange(lengths_row.shape[0], dtype=jnp.int32)
    start_of = jnp.sum(
        jnp.where(segment[:, None] == slot_ids[None, :], doc_starts[None, :], 0), axis=1
    )
    return (segment, row_index - start_of)


def rope_tables(position, head_width):
    half_dim = head_width // 2
    pair_ids = jnp.arange(half_dim, dtype=jnp.float32)
    inverse = jnp.exp(pair_ids * (-2.0 * math.log(ROPE_BASE) / head_width))
    angles = position.astype(jnp.float32)[:, None] * inverse[None, :]
    return (jnp.cos(angles)[:, None, :], jnp.sin(angles)[:, None, :])


def rotate(vectors, position):
    half_dim = vectors.shape[-1] // 2
    cosine, sine = rope_tables(position, vectors.shape[-1])
    first = vectors[..., :half_dim]
    second = vectors[..., half_dim:]
    return jnp.concatenate(
        [first * cosine - second * sine, second * cosine + first * sine], axis=-1
    )


def rotate_back(grads_in, position):
    half_dim = grads_in.shape[-1] // 2
    cosine, sine = rope_tables(position, grads_in.shape[-1])
    first = grads_in[..., :half_dim]
    second = grads_in[..., half_dim:]
    return jnp.concatenate(
        [first * cosine + second * sine, second * cosine - first * sine], axis=-1
    )


def heads_first(tensor_in):
    return jnp.moveaxis(tensor_in, 1, 0)


def forward_kernel(q_ref, k_ref, v_ref, seg_col_ref, seg_row_ref, out_ref, log_ref):
    scores = lax.dot_general(
        q_ref[0], k_ref[0], (((1,), (1,)), ((), ())), preferred_element_type=jnp.float32
    )
    scores = jnp.where(seg_col_ref[...] == seg_row_ref[...], scores, MASKED_SCORE)
    peak = jnp.max(scores, axis=-1, keepdims=True)
    weights = jnp.exp(scores - peak)
    total = jnp.sum(weights, axis=-1, keepdims=True)
    result = jnp.dot(
        weights.astype(jnp.bfloat16), v_ref[0], preferred_element_type=jnp.float32
    )
    out_ref[0] = (result / total).astype(jnp.bfloat16)
    log_ref[0] = peak + jnp.log(total)


def attention_forward(queries, key_rows, value_rows, segment, block_len):
    heads, rows, dim = queries.shape
    return pl.pallas_call(
        forward_kernel,
        grid=(heads, rows // block_len),
        in_specs=[
            pl.BlockSpec((1, block_len, dim), lambda h, b: (h, b, 0)),
            pl.BlockSpec((1, rows, dim), lambda h, b: (h, 0, 0)),
            pl.BlockSpec((1, rows, dim), lambda h, b: (h, 0, 0)),
            pl.BlockSpec((block_len, 1), lambda h, b: (b, 0)),
            pl.BlockSpec((1, rows), lambda h, b: (0, 0)),
        ],
        out_specs=[
            pl.BlockSpec((1, block_len, dim), lambda h, b: (h, b, 0)),
            pl.BlockSpec((1, block_len, 1), lambda h, b: (h, b, 0)),
        ],
        out_shape=[
            jax.ShapeDtypeStruct((heads, rows, dim), jnp.bfloat16),
            jax.ShapeDtypeStruct((heads, rows, 1), jnp.float32),
        ],
        compiler_params=pltpu.CompilerParams(vmem_limit_bytes=VMEM_BYTES),
        cost_estimate=pl.CostEstimate(
            flops=heads * rows * rows * dim * 16, bytes_accessed=heads * rows * dim * 8,
            transcendentals=heads * rows * rows,
        ),
    )(queries, key_rows, value_rows, segment[:, None], segment[None, :])


def backward_kernel(
    q_ref, k_ref, v_ref, g_ref, log_ref, delta_ref, seg_col_ref, seg_row_ref,
    dq_ref, dk_ref, dv_ref,
):
    keys = k_ref[0]
    query = q_ref[0]
    grad = g_ref[0]
    wide = (((1,), (1,)), ((), ()))
    scores = lax.dot_general(keys, query, wide, preferred_element_type=jnp.float32)
    scores = jnp.where(seg_col_ref[...] == seg_row_ref[...], scores - log_ref[0], MASKED_SCORE)
    weights = jnp.exp(scores)
    grad_weights = lax.dot_general(v_ref[0], grad, wide, preferred_element_type=jnp.float32)
    grad_scores = (weights * (grad_weights - delta_ref[0])).astype(jnp.bfloat16)
    part_v = jnp.dot(weights.astype(jnp.bfloat16), grad, preferred_element_type=jnp.float32)
    part_k = jnp.dot(grad_scores, query, preferred_element_type=jnp.float32)
    dq_ref[0] = lax.dot_general(
        grad_scores, keys, (((0,), (0,)), ((), ())), preferred_element_type=jnp.float32
    )

    @pl.when(pl.program_id(1) == 0)
    def _():
        dk_ref[0] = part_k
        dv_ref[0] = part_v

    @pl.when(pl.program_id(1) > 0)
    def _():
        dk_ref[0] += part_k
        dv_ref[0] += part_v


def attention_backward(queries, key_rows, value_rows, grads, logs, delta, segment, block_len):
    heads, rows, dim = queries.shape
    block = pl.BlockSpec((1, block_len, dim), lambda h, b: (h, b, 0))
    whole = pl.BlockSpec((1, rows, dim), lambda h, b: (h, 0, 0))
    line = pl.BlockSpec((1, 1, block_len), lambda h, b: (h, 0, b))
    result = jax.ShapeDtypeStruct((heads, rows, dim), jnp.float32)
    return pl.pallas_call(
        backward_kernel,
        grid=(heads, rows // block_len),
        in_specs=[
            block, whole, whole, block, line, line,
            pl.BlockSpec((rows, 1), lambda h, b: (0, 0)),
            pl.BlockSpec((1, block_len), lambda h, b: (0, b)),
        ],
        out_specs=[block, whole, whole],
        out_shape=[result, result, result],
        compiler_params=pltpu.CompilerParams(vmem_limit_bytes=VMEM_BYTES),
        cost_estimate=pl.CostEstimate(
            flops=heads * rows * rows * dim * 40, bytes_accessed=heads * rows * dim * 20,
            transcendentals=heads * rows * rows,
        ),
    )(
        queries, key_rows, value_rows, grads, logs[:, None, :], delta[:, None, :],
        segment[:, None], segment[None, :],
    )


def summed_over_both(grad, dp_dim, tensor_dim):
    over_dp = sent_and_summed(grad.astype(jnp.bfloat16), "dp", dp_dim)
    return sent_and_summed(over_dp.astype(jnp.bfloat16), "tensor", tensor_dim)


def gathered_over_both(weight, dp_dim, tensor_dim):
    over_tensor = lax.all_gather(weight, "tensor", axis=tensor_dim, tiled=True)
    return lax.all_gather(over_tensor, "dp", axis=dp_dim, tiled=True)


def per_device(layer_input, cotangent, lengths, w_qkv, w_out, w_in, w_down, attn_gain, mlp_gain):
    row_count, width = layer_input.shape
    group_rows = row_count * lax.axis_size("tensor")
    gathered_input = lax.all_gather(layer_input, "tensor", axis=0, tiled=True)
    both_gains = lax.all_gather(
        jnp.stack([attn_gain, mlp_gain]), "dp", axis=1, tiled=True
    ).astype(jnp.float32)
    gain_one, gain_two = both_gains[0], both_gains[1]
    full_qkv = lax.all_gather(w_qkv, "dp", axis=0, tiled=True)
    full_out = gathered_over_both(w_out, 1, 0)
    full_in = gathered_over_both(w_in, 0, 2)
    full_down = gathered_over_both(w_down, 1, 0)
    local_heads = full_qkv.shape[2] // HEAD_DIM
    segment, position = layout(lengths[0], group_rows)
    input_float = layer_input.astype(jnp.float32)
    gathered_one = layer_norm(gathered_input.astype(jnp.float32), gain_one).astype(jnp.bfloat16)
    flat_qkv = full_qkv.reshape(width, -1)
    projected = jnp.dot(gathered_one, flat_qkv, preferred_element_type=jnp.float32)
    projected = projected.reshape(group_rows, 3, local_heads, HEAD_DIM)
    factor = HEAD_DIM ** (-0.5)
    queries = heads_first((rotate(projected[:, 0], position) * factor).astype(jnp.bfloat16))
    key_rows = heads_first(rotate(projected[:, 1], position).astype(jnp.bfloat16))
    value_rows = heads_first(projected[:, 2].astype(jnp.bfloat16))
    head_out, head_logs = attention_forward(queries, key_rows, value_rows, segment, FORWARD_BLOCK)
    mixed_heads = jnp.moveaxis(head_out, 0, 1).reshape(group_rows, -1)
    mixed = lax.all_to_all(mixed_heads, "tensor", split_axis=0, concat_axis=1, tiled=True)
    attention = jnp.dot(mixed, full_out, preferred_element_type=jnp.float32)
    hidden = input_float + attention
    normed_two = layer_norm(hidden, gain_two).astype(jnp.bfloat16)
    unit_count = full_down.shape[0]
    flat_in = full_in.reshape(width, -1)
    gate_up = jnp.dot(normed_two, flat_in, preferred_element_type=jnp.float32).reshape(
        -1, 2, unit_count
    )
    activated = (jax.nn.gelu(gate_up[:, 0], approximate=False) * gate_up[:, 1]).astype(jnp.bfloat16)
    branch = jnp.dot(activated, full_down, preferred_element_type=jnp.float32)
    output = (hidden + branch).astype(jnp.bfloat16)
    grad_out = cotangent.astype(jnp.float32)
    grad_act = jnp.einsum("nd,ud->nu", cotangent, full_down, preferred_element_type=jnp.float32)
    grad_down = jnp.einsum("nu,nd->ud", activated, cotangent, preferred_element_type=jnp.float32)

    def gated(first_part, second_part):
        return jax.nn.gelu(first_part, approximate=False) * second_part

    unused_gated, gate_pullback = jax.vjp(gated, gate_up[:, 0], gate_up[:, 1])
    grad_first, grad_second = gate_pullback(grad_act)
    grad_gate_up = jnp.concatenate(
        [grad_first.astype(jnp.bfloat16), grad_second.astype(jnp.bfloat16)], axis=1
    )
    grad_in = jnp.einsum(
        "nd,nc->dc", normed_two, grad_gate_up, preferred_element_type=jnp.float32
    ).reshape(width, 2, unit_count)
    grad_two = jnp.einsum("nc,dc->nd", grad_gate_up, flat_in, preferred_element_type=jnp.float32)
    unused_second, second_pullback = jax.vjp(layer_norm, hidden, gain_two)
    grad_from_norm, grad_gain_two = second_pullback(grad_two)
    grad_hidden = grad_out + grad_from_norm
    grad_hidden_low = grad_hidden.astype(jnp.bfloat16)
    grad_mixed_rows = jnp.einsum(
        "nd,cd->nc", grad_hidden_low, full_out, preferred_element_type=jnp.float32
    ).astype(jnp.bfloat16)
    grad_mixed = lax.all_to_all(
        grad_mixed_rows, "tensor", split_axis=1, concat_axis=0, tiled=True
    )
    grad_w_out = jnp.einsum("nc,nd->cd", mixed, grad_hidden_low, preferred_element_type=jnp.float32)
    part_in = summed_over_both(grad_in, 0, 2)
    part_down = summed_over_both(grad_down, 1, 0)
    part_out = summed_over_both(grad_w_out, 1, 0)
    grad_heads = heads_first(grad_mixed.reshape(group_rows, local_heads, HEAD_DIM))
    delta = jnp.sum(grad_heads.astype(jnp.float32) * head_out.astype(jnp.float32), axis=-1)
    grad_q, grad_k, grad_v = attention_backward(
        queries, key_rows, value_rows, grad_heads, head_logs[..., 0], delta, segment,
        BACKWARD_BLOCK,
    )
    grad_query = rotate_back(heads_first(grad_q) * factor, position).astype(jnp.bfloat16)
    grad_key = rotate_back(heads_first(grad_k), position).astype(jnp.bfloat16)
    grad_value = heads_first(grad_v).astype(jnp.bfloat16)
    grad_proj = jnp.stack([grad_query, grad_key, grad_value], axis=1).reshape(group_rows, -1)
    grad_one_part = jnp.einsum(
        "nc,dc->nd", grad_proj, flat_qkv, preferred_element_type=jnp.float32
    )
    grad_one = lax.psum_scatter(
        grad_one_part.astype(jnp.bfloat16), "tensor", scatter_dimension=0, tiled=True
    ).astype(jnp.float32)
    grad_qkv = jnp.einsum(
        "nd,nc->dc", gathered_one, grad_proj, preferred_element_type=jnp.float32
    ).reshape(width, 3, -1)
    part_qkv = sent_and_summed(grad_qkv.astype(jnp.bfloat16), "dp", 0)
    unit_rows = layer_norm(gathered_input.astype(jnp.float32), 1.0)
    grad_gain_one = jnp.sum(grad_one_part * unit_rows, axis=0)
    both_parts = jnp.stack([grad_gain_one, grad_gain_two], axis=1)
    shares = sent_and_summed(both_parts, ("dp", "tensor"), 0)
    unused_first, first_pullback = jax.vjp(lambda rows: layer_norm(rows, gain_one), input_float)
    (grad_from_first,) = first_pullback(grad_one)
    grad_input = grad_hidden + grad_from_first
    return (
        output, grad_input, part_qkv, part_out, part_in, part_down, shares[:, 0], shares[:, 1]
    )


def solution(mesh):
    placed = (
        P(("dp", "tensor"), None),
        P(("dp", "tensor"), None),
        P("dp", None),
        P("dp", None, "tensor"),
        P("tensor", "dp"),
        P("dp", None, "tensor"),
        P("tensor", "dp"),
        P("dp"),
        P("dp"),
    )
    return jax.shard_map(
        per_device,
        mesh=mesh,
        in_specs=placed,
        out_specs=(
            P(("dp", "tensor"), None),
            P(("dp", "tensor"), None),
            P("dp", None, "tensor"),
            P("tensor", "dp"),
            P("dp", None, "tensor"),
            P("tensor", "dp"),
            P(("dp", "tensor")),
            P(("dp", "tensor")),
        ),
        check_vma=False,
    )
```

```python
import math

import jax
import jax.numpy as jnp
from jax import lax
from jax.experimental import pallas as pl
from jax.experimental.pallas import tpu as pltpu
from jax.sharding import PartitionSpec as P

HEAD_DIM = 64


NORM_EPS = 1e-05
ROPE_BASE = 160000.0
MASKED_SCORE = -1e30
VMEM_BYTES = 48 * 1024 * 1024
FORWARD_BLOCK = 512
BACKWARD_BLOCK = 512


def in_blocks(shard, dim, size):
    shape = shard.shape
    parts = shard.reshape(*shape[:dim], size, shape[dim] // size, *shape[dim + 1 :])
    return jnp.moveaxis(parts, dim, 0)


def sent_and_summed(shard, axis, dim):
    parts = in_blocks(shard, dim, lax.axis_size(axis))
    arrived = lax.all_to_all(parts, axis, split_axis=0, concat_axis=0, tiled=True)
    return arrived.astype(jnp.float32).sum(axis=0)


def layer_norm(values_in, gain):
    center = jnp.mean(values_in, axis=-1, keepdims=True)
    shifted = values_in - center
    spread = jnp.mean(shifted * shifted, axis=-1, keepdims=True)
    return shifted * lax.rsqrt(spread + NORM_EPS) * gain


def layout(lengths_row, row_count):
    doc_ends = jnp.cumsum(lengths_row)
    doc_starts = doc_ends - lengths_row
    row_index = jnp.arange(row_count, dtype=jnp.int32)
    segment = jnp.sum((row_index[:, None] >= doc_ends[None, :]).astype(jnp.int32), axis=1)
    slot_ids = jnp.arange(lengths_row.shape[0], dtype=jnp.int32)
    start_of = jnp.sum(
        jnp.where(segment[:, None] == slot_ids[None, :], doc_starts[None, :], 0), axis=1
    )
    return (segment, row_index - start_of)


WIDE = (((1,), (1,)), ((), ()))
DEEP = (((0,), (0,)), ((), ()))


def rope_tables(position):
    half_dim = HEAD_DIM // 2
    pair_ids = (jnp.arange(2 * HEAD_DIM, dtype=jnp.int32) % half_dim).astype(jnp.float32)
    inverse = jnp.exp(pair_ids * (-2.0 * math.log(ROPE_BASE) / HEAD_DIM))
    angles = position.astype(jnp.float32)[:, None] * inverse[None, :]
    return (jnp.cos(angles), jnp.sin(angles))


def halves_swapped(columns):
    pairs = columns.reshape(*columns.shape[:-1], -1, 2, HEAD_DIM // 2)
    swapped = jnp.stack([-pairs[..., 1, :], pairs[..., 0, :]], axis=-2)
    return swapped.reshape(columns.shape)


def turned_back(grads_in, cosine, sine):
    half_dim = HEAD_DIM // 2
    swapped = jnp.concatenate([grads_in[:, half_dim:], -grads_in[:, :half_dim]], axis=1)
    return grads_in * cosine + swapped * sine


def head_columns(part, head):
    return slice(part + head * HEAD_DIM, part + (head + 1) * HEAD_DIM)


def forward_kernel(q_ref, k_ref, v_ref, seg_col_ref, seg_row_ref, out_ref, log_ref):
    columns = v_ref.shape[1]
    allowed = seg_col_ref[...] == seg_row_ref[...]
    for head in range(columns // HEAD_DIM):
        own = head_columns(0, head)
        scores = lax.dot_general(
            k_ref[:, head_columns(columns, head)], q_ref[:, own], WIDE,
            preferred_element_type=jnp.float32,
        )
        scores = jnp.where(allowed, scores, MASKED_SCORE)
        peak = jnp.max(scores, axis=0, keepdims=True)
        weights = jnp.exp(scores - peak)
        total = jnp.sum(weights, axis=0, keepdims=True)
        weights = (weights * (1.0 / total)).astype(jnp.bfloat16)
        result = lax.dot_general(
            weights, v_ref[:, own], DEEP, preferred_element_type=jnp.float32
        )
        out_ref[:, own] = result.astype(jnp.bfloat16)
        log_ref[head : head + 1, :] = peak + jnp.log(total)


def attention_forward(query_key, values, segment, block_len):
    rows, columns = values.shape
    heads = columns // HEAD_DIM
    return pl.pallas_call(
        forward_kernel,
        grid=(rows // block_len,),
        in_specs=[
            pl.BlockSpec((block_len, 2 * columns), lambda b: (b, 0)),
            pl.BlockSpec((rows, 2 * columns), lambda b: (0, 0)),
            pl.BlockSpec((rows, columns), lambda b: (0, 0)),
            pl.BlockSpec((rows, 1), lambda b: (0, 0)),
            pl.BlockSpec((1, block_len), lambda b: (0, b)),
        ],
        out_specs=[
            pl.BlockSpec((block_len, columns), lambda b: (b, 0)),
            pl.BlockSpec((heads, block_len), lambda b: (0, b)),
        ],
        out_shape=[
            jax.ShapeDtypeStruct((rows, columns), jnp.bfloat16),
            jax.ShapeDtypeStruct((heads, rows), jnp.float32),
        ],
        compiler_params=pltpu.CompilerParams(vmem_limit_bytes=VMEM_BYTES),
        cost_estimate=pl.CostEstimate(
            flops=rows * rows * columns * 24, bytes_accessed=rows * columns * 8,
            transcendentals=heads * rows * rows,
        ),
    )(query_key, query_key, values, segment[:, None], segment[None, :])


def backward_kernel(
    q_ref, k_ref, v_ref, g_ref, out_ref, log_ref, seg_col_ref, seg_row_ref, cos_ref, sin_ref,
    d_ref, dk_ref, dv_ref,
):
    step = pl.program_id(0)
    columns = v_ref.shape[1]
    block_len = g_ref.shape[0]
    heads = columns // HEAD_DIM
    allowed = seg_col_ref[...] == seg_row_ref[...]
    own_rows = pl.ds(pl.multiple_of(step * block_len, block_len), block_len)
    ones = jnp.ones((8, HEAD_DIM), jnp.float32)

    @pl.when(step == 0)
    def _():
        dk_ref[...] = jnp.zeros_like(dk_ref)
        dv_ref[...] = jnp.zeros_like(dv_ref)

    for head in range(heads):
        own = head_columns(0, head)
        keys = k_ref[:, head_columns(columns, head)]
        query = q_ref[:, own]
        grad = g_ref[:, own]
        products = grad.astype(jnp.float32) * out_ref[:, own].astype(jnp.float32)
        delta = lax.dot_general(
            ones, products, WIDE, precision=lax.Precision.HIGHEST,
            preferred_element_type=jnp.float32,
        )[:1]
        scores = lax.dot_general(keys, query, WIDE, preferred_element_type=jnp.float32)
        scores = jnp.where(allowed, scores - log_ref[head : head + 1, :], MASKED_SCORE)
        weights = jnp.exp(scores)
        grad_weights = lax.dot_general(
            v_ref[:, own], grad, WIDE, preferred_element_type=jnp.float32
        )
        grad_scores = (weights * (grad_weights - delta)).astype(jnp.bfloat16)
        dv_ref[head] += jnp.dot(
            weights.astype(jnp.bfloat16), grad, preferred_element_type=jnp.float32
        )
        dk_ref[head] += jnp.dot(grad_scores, query, preferred_element_type=jnp.float32)
        grad_query = lax.dot_general(
            grad_scores, keys, DEEP, preferred_element_type=jnp.float32
        ) * (HEAD_DIM ** (-0.5))
        d_ref[own_rows, own] = turned_back(
            grad_query, cos_ref[own_rows, :HEAD_DIM], sin_ref[own_rows, :HEAD_DIM]
        ).astype(jnp.bfloat16)

    @pl.when(step == pl.num_programs(0) - 1)
    def _():
        for head in range(heads):
            d_ref[:, head_columns(columns, head)] = turned_back(
                dk_ref[head], cos_ref[:, :HEAD_DIM], sin_ref[:, :HEAD_DIM]
            ).astype(jnp.bfloat16)
            d_ref[:, head_columns(2 * columns, head)] = dv_ref[head].astype(jnp.bfloat16)


def attention_backward(query_key, values, grads, outs, logs, segment, cosine, sine, block_len):
    rows, columns = values.shape
    heads = columns // HEAD_DIM
    block = pl.BlockSpec((block_len, columns), lambda b: (b, 0))
    table = pl.BlockSpec((rows, 2 * HEAD_DIM), lambda b: (0, 0))
    return pl.pallas_call(
        backward_kernel,
        grid=(rows // block_len,),
        in_specs=[
            pl.BlockSpec((block_len, 2 * columns), lambda b: (b, 0)),
            pl.BlockSpec((rows, 2 * columns), lambda b: (0, 0)),
            pl.BlockSpec((rows, columns), lambda b: (0, 0)),
            block,
            block,
            pl.BlockSpec((heads, block_len), lambda b: (0, b)),
            pl.BlockSpec((rows, 1), lambda b: (0, 0)),
            pl.BlockSpec((1, block_len), lambda b: (0, b)),
            table,
            table,
        ],
        out_specs=pl.BlockSpec((rows, 3 * columns), lambda b: (0, 0)),
        out_shape=jax.ShapeDtypeStruct((rows, 3 * columns), jnp.bfloat16),
        scratch_shapes=[
            pltpu.VMEM((heads, rows, HEAD_DIM), jnp.float32),
            pltpu.VMEM((heads, rows, HEAD_DIM), jnp.float32),
        ],
        compiler_params=pltpu.CompilerParams(vmem_limit_bytes=VMEM_BYTES),
        cost_estimate=pl.CostEstimate(
            flops=rows * rows * columns * 40, bytes_accessed=rows * columns * 20,
            transcendentals=heads * rows * rows,
        ),
    )(
        query_key, query_key, values, grads, outs, logs, segment[:, None], segment[None, :],
        cosine, sine,
    )


def in_parts(packed, sizes):
    parts, start = [], 0
    for size in sizes:
        parts.append(packed[..., start : start + size])
        start += size
    return parts


def per_device(layer_input, cotangent, lengths, w_qkv, w_out, w_in, w_down, attn_gain, mlp_gain):
    row_count, width = layer_input.shape
    ways = lax.axis_size("tensor")
    group_rows = row_count * ways
    own_width = w_in.shape[0]
    own_units, own_columns = w_down.shape[0], w_out.shape[0]
    units = own_units * ways
    gathered_input = lax.all_gather(layer_input, "tensor", axis=0, tiled=True)
    own_pack = jnp.concatenate([w_in.reshape(own_width, -1), w_down.T, w_out.T], axis=1)
    tensor_pack = lax.all_gather(own_pack, "tensor", axis=0)
    pack_in, pack_down, pack_out = in_parts(tensor_pack, (2 * own_units, own_units, own_columns))
    dp_pack = jnp.concatenate(
        [
            jnp.transpose(
                pack_in.reshape(ways, own_width, 2, own_units), (1, 2, 0, 3)
            ).reshape(own_width, -1),
            jnp.moveaxis(pack_down, 0, 1).reshape(own_width, -1),
            jnp.moveaxis(pack_out, 0, 1).reshape(own_width, -1),
        ],
        axis=1,
    )
    both_gains = lax.all_gather(
        jnp.stack([attn_gain, mlp_gain]), "dp", axis=1, tiled=True
    ).astype(jnp.float32)
    gain_one, gain_two = both_gains[0], both_gains[1]
    flat_qkv = lax.all_gather(w_qkv.reshape(own_width, -1), "dp", axis=0, tiled=True)
    segment, position = layout(lengths[0], group_rows)
    cosine, sine = rope_tables(position)
    rotating, swapped_rotating = flat_qkv[:, : 2 * own_columns], halves_swapped(
        flat_qkv[:, : 2 * own_columns]
    )
    gathered_input, dp_pack, cosine, sine, swapped_rotating = lax.optimization_barrier(
        (gathered_input, dp_pack, cosine, sine, swapped_rotating)
    )
    full_pack = lax.all_gather(dp_pack, "dp", axis=0, tiled=True)
    input_float = layer_input.astype(jnp.float32)
    gathered_one = layer_norm(gathered_input.astype(jnp.float32), gain_one).astype(jnp.bfloat16)
    copies = own_columns // HEAD_DIM
    straight = jnp.dot(gathered_one, rotating, preferred_element_type=jnp.float32)
    swapped = jnp.dot(gathered_one, swapped_rotating, preferred_element_type=jnp.float32)
    scale = jnp.where(jnp.arange(2 * own_columns) < own_columns, HEAD_DIM ** (-0.5), 1.0)
    query_key = (
        (
            straight * jnp.concatenate([cosine] * copies, axis=1)
            + swapped * jnp.concatenate([sine] * copies, axis=1)
        )
        * scale
    ).astype(jnp.bfloat16)
    values = jnp.dot(
        gathered_one, flat_qkv[:, 2 * own_columns :], preferred_element_type=jnp.float32
    ).astype(jnp.bfloat16)
    mixed_heads, head_logs = attention_forward(query_key, values, segment, FORWARD_BLOCK)
    mixed = lax.all_to_all(
        mixed_heads.reshape(ways, row_count, own_columns), "tensor", split_axis=0, concat_axis=0
    )
    mixed = jnp.moveaxis(mixed, 0, 1).reshape(row_count, -1)
    flat_in, down_turned, out_turned = in_parts(full_pack, (2 * units, units, own_columns * ways))
    attention = lax.dot_general(mixed, out_turned, WIDE, preferred_element_type=jnp.float32)
    hidden = input_float + attention
    normed_two = layer_norm(hidden, gain_two).astype(jnp.bfloat16)
    gate_up = jnp.dot(normed_two, flat_in, preferred_element_type=jnp.float32)
    grad_act = jnp.dot(cotangent, down_turned, preferred_element_type=jnp.float32)

    def gated(first_part, second_part):
        return jax.nn.gelu(first_part, approximate=False) * second_part

    activated, gate_pullback = jax.vjp(gated, gate_up[:, :units], gate_up[:, units:])
    activated = activated.astype(jnp.bfloat16)
    grad_first, grad_second = gate_pullback(grad_act)
    grad_gate_up = jnp.concatenate(
        [grad_first.astype(jnp.bfloat16), grad_second.astype(jnp.bfloat16)], axis=1
    )
    grad_two = lax.dot_general(grad_gate_up, flat_in, WIDE, preferred_element_type=jnp.float32)
    unused_second, second_pullback = jax.vjp(layer_norm, hidden, gain_two)
    grad_from_norm, grad_gain_two = second_pullback(grad_two)
    grad_hidden = cotangent.astype(jnp.float32) + grad_from_norm
    grad_hidden_low = grad_hidden.astype(jnp.bfloat16)
    grad_mixed_rows = jnp.dot(
        grad_hidden_low, out_turned, preferred_element_type=jnp.float32
    ).astype(jnp.bfloat16)
    grad_mixed = lax.all_to_all(
        jnp.moveaxis(grad_mixed_rows.reshape(row_count, ways, own_columns), 1, 0),
        "tensor", split_axis=0, concat_axis=0,
    ).reshape(group_rows, own_columns)
    branch = lax.dot_general(activated, down_turned, WIDE, preferred_element_type=jnp.float32)
    output = (hidden + branch).astype(jnp.bfloat16)
    weight_grads = jnp.concatenate(
        [
            lax.dot_general(left, right, DEEP, preferred_element_type=jnp.float32).astype(
                jnp.bfloat16
            )
            for left, right in (
                (normed_two, grad_gate_up), (cotangent, activated), (grad_hidden_low, mixed)
            )
        ],
        axis=1,
    )
    grad_mixed, weight_grads, output = lax.optimization_barrier(
        (grad_mixed, weight_grads, output)
    )
    over_dp = sent_and_summed(weight_grads, "dp", 0).astype(jnp.bfloat16)
    grad_proj = attention_backward(
        query_key, values, grad_mixed, mixed_heads, head_logs, segment, cosine, sine,
        BACKWARD_BLOCK,
    )
    grad_one_part = lax.dot_general(grad_proj, flat_qkv, WIDE, preferred_element_type=jnp.float32)
    grad_one = lax.psum_scatter(
        grad_one_part.astype(jnp.bfloat16), "tensor", scatter_dimension=0, tiled=True
    ).astype(jnp.float32)
    grad_qkv = lax.dot_general(gathered_one, grad_proj, DEEP, preferred_element_type=jnp.float32)
    part_qkv = sent_and_summed(grad_qkv.astype(jnp.bfloat16), "dp", 0).reshape(w_qkv.shape)
    dp_in, dp_down, dp_out = in_parts(over_dp, (2 * units, units, own_columns * ways))
    to_send = jnp.concatenate(
        [
            jnp.transpose(
                dp_in.reshape(own_width, 2, ways, own_units), (2, 0, 1, 3)
            ).reshape(ways, own_width, -1),
            jnp.moveaxis(dp_down.reshape(own_width, ways, -1), 1, 0),
            jnp.moveaxis(dp_out.reshape(own_width, ways, -1), 1, 0),
        ],
        axis=2,
    )
    over_both = lax.all_to_all(to_send, "tensor", split_axis=0, concat_axis=0)
    over_both = over_both.astype(jnp.float32).sum(axis=0)
    part_in, part_down, part_out = in_parts(over_both, (2 * own_units, own_units, own_columns))
    unit_rows = layer_norm(gathered_input.astype(jnp.float32), 1.0)
    grad_gain_one = jnp.sum(grad_one_part * unit_rows, axis=0)
    both_parts = jnp.stack([grad_gain_one, grad_gain_two], axis=1)
    shares = sent_and_summed(both_parts, ("dp", "tensor"), 0)
    unused_first, first_pullback = jax.vjp(lambda rows: layer_norm(rows, gain_one), input_float)
    (grad_from_first,) = first_pullback(grad_one)
    grad_input = grad_hidden + grad_from_first
    return (
        output, grad_input, part_qkv, part_out.T, part_in.reshape(w_in.shape), part_down.T,
        shares[:, 0], shares[:, 1],
    )


def solution(mesh):
    placed = (
        P(("dp", "tensor"), None),
        P(("dp", "tensor"), None),
        P("dp", None),
        P("dp", None, "tensor"),
        P("tensor", "dp"),
        P("dp", None, "tensor"),
        P("tensor", "dp"),
        P("dp"),
        P("dp"),
    )
    return jax.shard_map(
        per_device,
        mesh=mesh,
        in_specs=placed,
        out_specs=(
            P(("dp", "tensor"), None),
            P(("dp", "tensor"), None),
            P("dp", None, "tensor"),
            P("tensor", "dp"),
            P("dp", None, "tensor"),
            P("tensor", "dp"),
            P(("dp", "tensor")),
            P(("dp", "tensor")),
        ),
        check_vma=False,
    )
```

```python
import math

import jax
import jax.numpy as jnp
from jax import lax
from jax.experimental import pallas as pl
from jax.experimental.pallas import tpu as pltpu
from jax.sharding import PartitionSpec as P

HEAD_DIM = 64


NORM_EPS = 1e-05
ROPE_BASE = 160000.0
MASKED_SCORE = -1e30
VMEM_BYTES = 48 * 1024 * 1024
FORWARD_BLOCK = 512
BACKWARD_BLOCK = 512


def in_blocks(shard, dim, size):
    shape = shard.shape
    parts = shard.reshape(*shape[:dim], size, shape[dim] // size, *shape[dim + 1 :])
    return jnp.moveaxis(parts, dim, 0)


def sent_and_summed(shard, axis, dim):
    parts = in_blocks(shard, dim, lax.axis_size(axis))
    arrived = lax.all_to_all(parts, axis, split_axis=0, concat_axis=0, tiled=True)
    return arrived.astype(jnp.float32).sum(axis=0)


def layer_norm(values_in, gain):
    center = jnp.mean(values_in, axis=-1, keepdims=True)
    shifted = values_in - center
    spread = jnp.mean(shifted * shifted, axis=-1, keepdims=True)
    return shifted * lax.rsqrt(spread + NORM_EPS) * gain


def layout(lengths_row, row_count):
    doc_ends = jnp.cumsum(lengths_row)
    doc_starts = doc_ends - lengths_row
    row_index = jnp.arange(row_count, dtype=jnp.int32)
    segment = jnp.sum((row_index[:, None] >= doc_ends[None, :]).astype(jnp.int32), axis=1)
    slot_ids = jnp.arange(lengths_row.shape[0], dtype=jnp.int32)
    start_of = jnp.sum(
        jnp.where(segment[:, None] == slot_ids[None, :], doc_starts[None, :], 0), axis=1
    )
    return (segment, row_index - start_of)


WIDE = (((1,), (1,)), ((), ()))
DEEP = (((0,), (0,)), ((), ()))


def rope_tables(position):
    half_dim = HEAD_DIM // 2
    pair_ids = (jnp.arange(2 * HEAD_DIM, dtype=jnp.int32) % half_dim).astype(jnp.float32)
    inverse = jnp.exp(pair_ids * (-2.0 * math.log(ROPE_BASE) / HEAD_DIM))
    angles = position.astype(jnp.float32)[:, None] * inverse[None, :]
    return (jnp.cos(angles), jnp.sin(angles))


def halves_swapped(columns):
    pairs = columns.reshape(*columns.shape[:-1], -1, 2, HEAD_DIM // 2)
    swapped = jnp.stack([-pairs[..., 1, :], pairs[..., 0, :]], axis=-2)
    return swapped.reshape(columns.shape)


def turned_back(grads_in, cosine, sine):
    half_dim = HEAD_DIM // 2
    swapped = jnp.concatenate([grads_in[:, half_dim:], -grads_in[:, :half_dim]], axis=1)
    return grads_in * cosine + swapped * sine


def head_columns(part, head):
    return slice(part + head * HEAD_DIM, part + (head + 1) * HEAD_DIM)


def forward_kernel(q_ref, k_ref, v_ref, seg_col_ref, seg_row_ref, out_ref, log_ref):
    columns = v_ref.shape[1]
    allowed = seg_col_ref[...] == seg_row_ref[...]
    for head in range(columns // HEAD_DIM):
        own = head_columns(0, head)
        scores = lax.dot_general(
            k_ref[:, head_columns(columns, head)], q_ref[:, own], WIDE,
            preferred_element_type=jnp.float32,
        )
        scores = jnp.where(allowed, scores, MASKED_SCORE)
        peak = jnp.max(scores, axis=0, keepdims=True)
        weights = jnp.exp(scores - peak)
        total = jnp.sum(weights, axis=0, keepdims=True)
        weights = (weights * (1.0 / total)).astype(jnp.bfloat16)
        result = lax.dot_general(
            weights, v_ref[:, own], DEEP, preferred_element_type=jnp.float32
        )
        out_ref[:, own] = result.astype(jnp.bfloat16)
        log_ref[head : head + 1, :] = peak + jnp.log(total)


def attention_forward(query_key, values, segment, block_len):
    rows, columns = values.shape
    heads = columns // HEAD_DIM
    return pl.pallas_call(
        forward_kernel,
        grid=(rows // block_len,),
        in_specs=[
            pl.BlockSpec((block_len, 2 * columns), lambda b: (b, 0)),
            pl.BlockSpec((rows, 2 * columns), lambda b: (0, 0)),
            pl.BlockSpec((rows, columns), lambda b: (0, 0)),
            pl.BlockSpec((rows, 1), lambda b: (0, 0)),
            pl.BlockSpec((1, block_len), lambda b: (0, b)),
        ],
        out_specs=[
            pl.BlockSpec((block_len, columns), lambda b: (b, 0)),
            pl.BlockSpec((heads, block_len), lambda b: (0, b)),
        ],
        out_shape=[
            jax.ShapeDtypeStruct((rows, columns), jnp.bfloat16),
            jax.ShapeDtypeStruct((heads, rows), jnp.float32),
        ],
        compiler_params=pltpu.CompilerParams(vmem_limit_bytes=VMEM_BYTES),
        cost_estimate=pl.CostEstimate(
            flops=rows * rows * columns * 24, bytes_accessed=rows * columns * 8,
            transcendentals=heads * rows * rows,
        ),
    )(query_key, query_key, values, segment[:, None], segment[None, :])


def backward_kernel(
    q_ref, k_ref, v_ref, g_ref, out_ref, log_ref, seg_col_ref, seg_row_ref, cos_ref, sin_ref,
    d_ref, dk_ref, dv_ref,
):
    step = pl.program_id(0)
    columns = v_ref.shape[1]
    block_len = g_ref.shape[0]
    heads = columns // HEAD_DIM
    allowed = seg_col_ref[...] == seg_row_ref[...]
    own_rows = pl.ds(pl.multiple_of(step * block_len, block_len), block_len)
    ones = jnp.ones((8, HEAD_DIM), jnp.float32)

    @pl.when(step == 0)
    def _():
        dk_ref[...] = jnp.zeros_like(dk_ref)
        dv_ref[...] = jnp.zeros_like(dv_ref)

    for head in range(heads):
        own = head_columns(0, head)
        keys = k_ref[:, head_columns(columns, head)]
        query = q_ref[:, own]
        grad = g_ref[:, own]
        products = grad.astype(jnp.float32) * out_ref[:, own].astype(jnp.float32)
        delta = lax.dot_general(
            ones, products, WIDE, precision=lax.Precision.HIGHEST,
            preferred_element_type=jnp.float32,
        )[:1]
        scores = lax.dot_general(keys, query, WIDE, preferred_element_type=jnp.float32)
        scores = jnp.where(allowed, scores - log_ref[head : head + 1, :], MASKED_SCORE)
        weights = jnp.exp(scores)
        grad_weights = lax.dot_general(
            v_ref[:, own], grad, WIDE, preferred_element_type=jnp.float32
        )
        grad_scores = (weights * (grad_weights - delta)).astype(jnp.bfloat16)
        dv_ref[head] += jnp.dot(
            weights.astype(jnp.bfloat16), grad, preferred_element_type=jnp.float32
        )
        dk_ref[head] += jnp.dot(grad_scores, query, preferred_element_type=jnp.float32)
        grad_query = lax.dot_general(
            grad_scores, keys, DEEP, preferred_element_type=jnp.float32
        ) * (HEAD_DIM ** (-0.5))
        d_ref[own_rows, own] = turned_back(
            grad_query, cos_ref[own_rows, :HEAD_DIM], sin_ref[own_rows, :HEAD_DIM]
        ).astype(jnp.bfloat16)

    @pl.when(step == pl.num_programs(0) - 1)
    def _():
        for head in range(heads):
            d_ref[:, head_columns(columns, head)] = turned_back(
                dk_ref[head], cos_ref[:, :HEAD_DIM], sin_ref[:, :HEAD_DIM]
            ).astype(jnp.bfloat16)
            d_ref[:, head_columns(2 * columns, head)] = dv_ref[head].astype(jnp.bfloat16)


def attention_backward(query_key, values, grads, outs, logs, segment, cosine, sine, block_len):
    rows, columns = values.shape
    heads = columns // HEAD_DIM
    block = pl.BlockSpec((block_len, columns), lambda b: (b, 0))
    table = pl.BlockSpec((rows, 2 * HEAD_DIM), lambda b: (0, 0))
    return pl.pallas_call(
        backward_kernel,
        grid=(rows // block_len,),
        in_specs=[
            pl.BlockSpec((block_len, 2 * columns), lambda b: (b, 0)),
            pl.BlockSpec((rows, 2 * columns), lambda b: (0, 0)),
            pl.BlockSpec((rows, columns), lambda b: (0, 0)),
            block,
            block,
            pl.BlockSpec((heads, block_len), lambda b: (0, b)),
            pl.BlockSpec((rows, 1), lambda b: (0, 0)),
            pl.BlockSpec((1, block_len), lambda b: (0, b)),
            table,
            table,
        ],
        out_specs=pl.BlockSpec((rows, 3 * columns), lambda b: (0, 0)),
        out_shape=jax.ShapeDtypeStruct((rows, 3 * columns), jnp.bfloat16),
        scratch_shapes=[
            pltpu.VMEM((heads, rows, HEAD_DIM), jnp.float32),
            pltpu.VMEM((heads, rows, HEAD_DIM), jnp.float32),
        ],
        compiler_params=pltpu.CompilerParams(vmem_limit_bytes=VMEM_BYTES),
        cost_estimate=pl.CostEstimate(
            flops=rows * rows * columns * 40, bytes_accessed=rows * columns * 20,
            transcendentals=heads * rows * rows,
        ),
    )(
        query_key, query_key, values, grads, outs, logs, segment[:, None], segment[None, :],
        cosine, sine,
    )


def in_parts(packed, sizes):
    parts, start = [], 0
    for size in sizes:
        parts.append(packed[..., start : start + size])
        start += size
    return parts


def per_device(layer_input, cotangent, lengths, w_qkv, w_out, w_in, w_down, attn_gain, mlp_gain):
    row_count, width = layer_input.shape
    ways = lax.axis_size("tensor")
    group_rows = row_count * ways
    own_width = w_in.shape[0]
    own_units, own_columns = w_down.shape[0], w_out.shape[0]
    units = own_units * ways
    gathered_input = lax.all_gather(layer_input, "tensor", axis=0, tiled=True)
    own_pack = jnp.concatenate([w_in.reshape(own_width, -1), w_down.T, w_out.T], axis=1)
    tensor_pack = lax.all_gather(own_pack, "tensor", axis=0)
    pack_in, pack_down, pack_out = in_parts(tensor_pack, (2 * own_units, own_units, own_columns))
    dp_pack = jnp.concatenate(
        [
            jnp.transpose(
                pack_in.reshape(ways, own_width, 2, own_units), (1, 2, 0, 3)
            ).reshape(own_width, -1),
            jnp.moveaxis(pack_down, 0, 1).reshape(own_width, -1),
            jnp.moveaxis(pack_out, 0, 1).reshape(own_width, -1),
        ],
        axis=1,
    )
    gain_columns = jnp.stack([attn_gain, mlp_gain], axis=1)
    gain_columns = jnp.pad(gain_columns, ((0, 0), (0, 126)))
    first_pack = lax.all_gather(
        jnp.concatenate([w_qkv.reshape(own_width, -1), gain_columns], axis=1),
        "dp", axis=0, tiled=True,
    )
    flat_qkv = first_pack[:, :-128]
    both_gains = first_pack[:, -128:-126].astype(jnp.float32).T
    gain_one, gain_two = both_gains[0], both_gains[1]
    segment, position = layout(lengths[0], group_rows)
    cosine, sine = rope_tables(position)
    rotating, swapped_rotating = flat_qkv[:, : 2 * own_columns], halves_swapped(
        flat_qkv[:, : 2 * own_columns]
    )
    gathered_input, dp_pack, cosine, sine, swapped_rotating = lax.optimization_barrier(
        (gathered_input, dp_pack, cosine, sine, swapped_rotating)
    )
    full_pack = lax.all_gather(dp_pack, "dp", axis=0, tiled=True)
    input_float = layer_input.astype(jnp.float32)
    gathered_one = layer_norm(gathered_input.astype(jnp.float32), gain_one).astype(jnp.bfloat16)
    copies = own_columns // HEAD_DIM
    straight = jnp.dot(gathered_one, rotating, preferred_element_type=jnp.float32)
    swapped = jnp.dot(gathered_one, swapped_rotating, preferred_element_type=jnp.float32)
    scale = jnp.where(jnp.arange(2 * own_columns) < own_columns, HEAD_DIM ** (-0.5), 1.0)
    query_key = (
        (
            straight * jnp.concatenate([cosine] * copies, axis=1)
            + swapped * jnp.concatenate([sine] * copies, axis=1)
        )
        * scale
    ).astype(jnp.bfloat16)
    values = jnp.dot(
        gathered_one, flat_qkv[:, 2 * own_columns :], preferred_element_type=jnp.float32
    ).astype(jnp.bfloat16)
    mixed_heads, head_logs = attention_forward(query_key, values, segment, FORWARD_BLOCK)
    mixed = lax.all_to_all(
        mixed_heads.reshape(ways, row_count, own_columns), "tensor", split_axis=0, concat_axis=0
    )
    mixed = jnp.moveaxis(mixed, 0, 1).reshape(row_count, -1)
    flat_in, down_turned, out_turned = in_parts(full_pack, (2 * units, units, own_columns * ways))
    attention = lax.dot_general(mixed, out_turned, WIDE, preferred_element_type=jnp.float32)
    hidden = input_float + attention
    normed_two = layer_norm(hidden, gain_two).astype(jnp.bfloat16)
    gate_up = jnp.dot(normed_two, flat_in, preferred_element_type=jnp.float32)
    grad_act = jnp.dot(cotangent, down_turned, preferred_element_type=jnp.float32)

    def gated(first_part, second_part):
        return jax.nn.gelu(first_part, approximate=False) * second_part

    activated, gate_pullback = jax.vjp(gated, gate_up[:, :units], gate_up[:, units:])
    activated = activated.astype(jnp.bfloat16)
    grad_first, grad_second = gate_pullback(grad_act)
    grad_gate_up = jnp.concatenate(
        [grad_first.astype(jnp.bfloat16), grad_second.astype(jnp.bfloat16)], axis=1
    )
    grad_two = lax.dot_general(grad_gate_up, flat_in, WIDE, preferred_element_type=jnp.float32)
    unused_second, second_pullback = jax.vjp(layer_norm, hidden, gain_two)
    grad_from_norm, grad_gain_two = second_pullback(grad_two)
    grad_hidden = cotangent.astype(jnp.float32) + grad_from_norm
    grad_hidden_low = grad_hidden.astype(jnp.bfloat16)
    grad_mixed_rows = jnp.dot(
        grad_hidden_low, out_turned, preferred_element_type=jnp.float32
    ).astype(jnp.bfloat16)
    grad_mixed = lax.all_to_all(
        jnp.moveaxis(grad_mixed_rows.reshape(row_count, ways, own_columns), 1, 0),
        "tensor", split_axis=0, concat_axis=0,
    ).reshape(group_rows, own_columns)
    branch = lax.dot_general(activated, down_turned, WIDE, preferred_element_type=jnp.float32)
    output = (hidden + branch).astype(jnp.bfloat16)
    grad_in, grad_down, grad_w_out = [
        lax.dot_general(left, right, DEEP, preferred_element_type=jnp.float32).astype(jnp.bfloat16)
        for left, right in (
            (normed_two, grad_gate_up), (cotangent, activated), (grad_hidden_low, mixed)
        )
    ]
    later_grads = jnp.concatenate([grad_down, grad_w_out], axis=1)
    grad_mixed, grad_in, later_grads, output = lax.optimization_barrier(
        (grad_mixed, grad_in, later_grads, output)
    )
    arrived_in = lax.all_to_all(
        in_blocks(grad_in, 0, lax.axis_size("dp")), "dp", split_axis=0, concat_axis=0
    )
    grad_proj = attention_backward(
        query_key, values, grad_mixed, mixed_heads, head_logs, segment, cosine, sine,
        BACKWARD_BLOCK,
    )
    grad_proj, arrived_in, later_grads = lax.optimization_barrier(
        (grad_proj, arrived_in, later_grads)
    )
    dp_in = arrived_in.astype(jnp.float32).sum(axis=0).astype(jnp.bfloat16)
    dp_later = sent_and_summed(later_grads, "dp", 0).astype(jnp.bfloat16)
    grad_one_part = lax.dot_general(grad_proj, flat_qkv, WIDE, preferred_element_type=jnp.float32)
    grad_one = lax.psum_scatter(
        grad_one_part.astype(jnp.bfloat16), "tensor", scatter_dimension=0, tiled=True
    ).astype(jnp.float32)
    grad_qkv = lax.dot_general(gathered_one, grad_proj, DEEP, preferred_element_type=jnp.float32)
    part_qkv = sent_and_summed(grad_qkv.astype(jnp.bfloat16), "dp", 0).reshape(w_qkv.shape)
    dp_down, dp_out = in_parts(dp_later, (units, own_columns * ways))
    to_send = jnp.concatenate(
        [
            jnp.transpose(
                dp_in.reshape(own_width, 2, ways, own_units), (2, 0, 1, 3)
            ).reshape(ways, own_width, -1),
            jnp.moveaxis(dp_down.reshape(own_width, ways, -1), 1, 0),
            jnp.moveaxis(dp_out.reshape(own_width, ways, -1), 1, 0),
        ],
        axis=2,
    )
    over_both = lax.all_to_all(to_send, "tensor", split_axis=0, concat_axis=0)
    over_both = over_both.astype(jnp.float32).sum(axis=0)
    part_in, part_down, part_out = in_parts(over_both, (2 * own_units, own_units, own_columns))
    unit_rows = layer_norm(gathered_input.astype(jnp.float32), 1.0)
    grad_gain_one = jnp.sum(grad_one_part * unit_rows, axis=0)
    both_parts = jnp.stack([grad_gain_one, grad_gain_two], axis=1)
    shares = sent_and_summed(both_parts, ("dp", "tensor"), 0)
    unused_first, first_pullback = jax.vjp(lambda rows: layer_norm(rows, gain_one), input_float)
    (grad_from_first,) = first_pullback(grad_one)
    grad_input = grad_hidden + grad_from_first
    return (
        output, grad_input, part_qkv, part_out.T, part_in.reshape(w_in.shape), part_down.T,
        shares[:, 0], shares[:, 1],
    )


def solution(mesh):
    placed = (
        P(("dp", "tensor"), None),
        P(("dp", "tensor"), None),
        P("dp", None),
        P("dp", None, "tensor"),
        P("tensor", "dp"),
        P("dp", None, "tensor"),
        P("tensor", "dp"),
        P("dp"),
        P("dp"),
    )
    return jax.shard_map(
        per_device,
        mesh=mesh,
        in_specs=placed,
        out_specs=(
            P(("dp", "tensor"), None),
            P(("dp", "tensor"), None),
            P("dp", None, "tensor"),
            P("tensor", "dp"),
            P("dp", None, "tensor"),
            P("tensor", "dp"),
            P(("dp", "tensor")),
            P(("dp", "tensor")),
        ),
        check_vma=False,
    )
```
